32 devices in a mesh: shard: 16 (over z, y, core), seq: 2 (over x).
Axes of the slice: x: 2, y: 2, z: 4, core: 2. Of those that a mesh axis runs over, the one named last changes fastest.
Arguments:
- tokens: bfloat16 [32, 1024, 1024], P('shard', 'seq'), may hold values from -6 to 6
- condition: bfloat16 [32, 1024], P('shard'), may hold values from -6 to 6
- cotangent: bfloat16 [32, 1024, 1024], P('shard', 'seq'), may hold values from -6 to 6
- ada_weight: bfloat16 [1024, 6144], P('shard'), may hold values from -0.1875 to 0.1875
- ada_bias: bfloat16 [6144], P('shard'), may hold values from -4 to 4
- qkv_weight: bfloat16 [1024, 3072], P('shard'), may hold values from -0.1875 to 0.1875
- qv_bias: bfloat16 [2048], P('shard'), may hold values from -3 to 3
- proj_weight: bfloat16 [1024, 1024], P('shard'), may hold values from -0.75 to 0.75
- proj_bias: bfloat16 [1024], P('shard'), may hold values from -3 to 3
- up_weight: bfloat16 [1024, 4096], P('shard'), may hold values from -0.1875 to 0.1875
- up_bias: bfloat16 [4096], P('shard'), may hold values from -3 to 3
- down_weight: bfloat16 [4096, 1024], P('shard'), may hold values from -0.09375 to 0.09375
- down_bias: bfloat16 [1024], P('shard'), may hold values from -3 to 3
Outputs:
- result: bfloat16 [32, 1024, 1024], P('shard', 'seq')
- grad_tokens: float32 [32, 1024, 1024], P('shard', 'seq')
- grad_condition: float32 [32, 1024], P('shard')
- grad_ada_weight: float32 [1024, 6144], P('shard')
- grad_ada_bias: float32 [6144], P('shard')
- grad_qkv_weight: float32 [1024, 3072], P('shard')
- grad_qv_bias: float32 [2048], P('shard')
- grad_proj_weight: float32 [1024, 1024], P('shard')
- grad_proj_bias: float32 [1024], P('shard')
- grad_up_weight: float32 [1024, 4096], P('shard')
- grad_up_bias: float32 [4096], P('shard')
- grad_down_weight: float32 [4096, 1024], P('shard')
- grad_down_bias: float32 [1024], P('shard')
The draws below stay inside these ranges and needn't reach their ends.
All inputs are finite; a program needn't handle non-finite values.
Results may differ from the reference program's by a relative error of at most 0.02.
The reference program's roundings to bfloat16 on the way count: a program that leaves them out, or rounds other values in their place, can miss the bound.
Values may be sent and summed in bfloat16 or wider, within the bound.
A program may use at most 320 MiB of HBM per device.

```python
import math
import jax
import jax.numpy as jnp
from jax import lax

D = 1024
HEADS = 16
HD = 64
FF = 4096
SEQ = 1024
LATENTS = 32


def block_scale(key, dims, pieces, least, high):
    def one(axis_at, blocks):
        steps = jax.random.uniform(jax.random.fold_in(jax.random.fold_in(key, 6), axis_at), (blocks,), jnp.float32, least / len(pieces), high / len(pieces))
        return jnp.repeat(jnp.exp(steps), dims[axis_at] // blocks).reshape((-1,) + (1,) * (len(dims) - axis_at - 1))

    gain = one(*pieces[0])
    for cut in pieces[1:]:
        gain = gain * one(*cut)
    return gain


def gaussian(key, extent, width, limit, cuts=(), held_as=jnp.bfloat16):
    values = width * jax.random.normal(key, extent, jnp.float32)
    if cuts:
        values = values * block_scale(key, extent, cuts, -0.22, 0.18)
    return jnp.clip(values, -limit, limit).astype(held_as)


def setup_inputs(seed: int = 0) -> dict:
    key_list = jax.random.split(jax.random.key(seed), 14)
    return {
        "tokens": gaussian(key_list[0], (LATENTS, SEQ, D), 1.0, 6.0, ((0, 16), (1, 2))),
        "condition": gaussian(key_list[1], (LATENTS, D), 1.0, 6.0, ((0, 16),)),
        "cotangent": gaussian(key_list[2], (LATENTS, SEQ, D), 1.0, 6.0, ((0, 16), (1, 2))),
        "ada_weight": gaussian(key_list[3], (D, 6 * D), D ** -0.5, 0.1875, ((0, 16),)),
        "ada_bias": gaussian(key_list[4], (6 * D,), 1.0, 4.0, ((0, 16),)),
        "qkv_weight": gaussian(key_list[5], (D, 3 * D), D ** -0.5, 0.1875, ((0, 16),)),
        "qv_bias": gaussian(key_list[6], (2 * D,), 0.5, 3.0, ((0, 16),)),
        "proj_weight": gaussian(key_list[7], (D, D), (D // 16) ** -0.5, 0.75, ((0, 16),)),
        "proj_bias": gaussian(key_list[8], (D,), 0.5, 3.0, ((0, 16),)),
        "up_weight": gaussian(key_list[9], (D, FF), D ** -0.5, 0.1875, ((0, 16),)),
        "up_bias": gaussian(key_list[10], (FF,), 0.5, 3.0, ((0, 16),)),
        "down_weight": gaussian(key_list[11], (FF, D), FF ** -0.5, 0.09375, ((0, 16),)),
        "down_bias": gaussian(key_list[12], (D,), 0.5, 3.0, ((0, 16),)),
    }


highest = lax.Precision.HIGHEST
epsilon = 1e-06

@jax.custom_vjp
def low(v):
    return lax.optimization_barrier(v.astype(jnp.bfloat16)).astype(jnp.float32)

@jax.custom_vjp
def low_back(v):
    return v

def low_keep(v):
    return (low(v), None)

def low_pass(kept, grad):
    return (grad,)

def back_keep(v):
    return (v, None)

def back_low(kept, grad):
    return (low(grad),)
low.defvjp(low_keep, low_pass)
low_back.defvjp(back_keep, back_low)

def modulate(residual, shift, scale):
    average = lax.optimization_barrier(jnp.mean(residual, -1, keepdims=True))
    centred = residual - average
    spread = lax.optimization_barrier(jnp.mean(centred * centred, -1, keepdims=True))
    return centred * lax.rsqrt(spread + epsilon) * (1.0 + scale) + shift

def attend(query_rows, key_rows, value_rows):
    length = query_rows.shape[0]
    factor = 1.0 / math.sqrt(HD)
    query_heads = query_rows.reshape(length, HEADS, HD)
    key_heads = key_rows.reshape(length, HEADS, HD)
    value_heads = value_rows.reshape(length, HEADS, HD)
    scores = low_back(jnp.einsum('qhd,khd->hqk', query_heads, key_heads, precision=highest) * factor)
    attn_probs = low(jax.nn.softmax(scores, axis=-1))
    combined = jnp.einsum('hqk,khd->qhd', attn_probs, value_heads, precision=highest)
    return combined.reshape(length, HEADS * HD)

def layer(residual, condition, ada_weight, ada_bias, qkv_weight, qv_bias, proj_weight, proj_bias, up_weight, up_bias, down_weight, down_bias):
    cond_act = low(jax.nn.silu(condition))
    modulation = low_back(jnp.dot(cond_act, ada_weight, precision=highest) + ada_bias)
    shift_one, scale_one, gate_one, shift_two, scale_two, gate_two = jnp.split(modulation, 6)
    normed_one = low(modulate(residual, shift_one, scale_one))
    project = jnp.dot(normed_one, qkv_weight, precision=highest)
    query_rows = low(low_back(project[:, :D] + qv_bias[:D]))
    key_rows = low(low_back(project[:, D:2 * D]))
    value_rows = low(low_back(project[:, 2 * D:] + qv_bias[D:]))
    attended = low(low_back(jax.checkpoint(attend)(query_rows, key_rows, value_rows)))
    branch = low_back(jnp.dot(attended, proj_weight, precision=highest) + proj_bias)
    middle = residual + gate_one * branch
    normed_two = low(modulate(middle, shift_two, scale_two))
    hidden = low_back(jnp.dot(normed_two, up_weight, precision=highest) + up_bias)
    active = low(jax.nn.gelu(hidden, approximate=True))
    output = low_back(jnp.dot(active, down_weight, precision=highest) + down_bias)
    return middle + gate_two * output

def reference(tokens, condition, cotangent, ada_weight, ada_bias, qkv_weight, qv_bias, proj_weight, proj_bias, up_weight, up_bias, down_weight, down_bias):
    params = tuple((weight.astype(jnp.float32) for weight in (ada_weight, ada_bias, qkv_weight, qv_bias, proj_weight, proj_bias, up_weight, up_bias, down_weight, down_bias)))

    def per_latent(running, sample):
        latent, cond_row, cot_rows = sample
        output, pullback = jax.vjp(layer, latent.astype(jnp.float32), cond_row.astype(jnp.float32), *params)
        gradients = pullback(cot_rows.astype(jnp.float32))
        running = tuple((total + gradient for total, gradient in zip(running, gradients[2:])))
        return (running, (output.astype(jnp.bfloat16), gradients[0], gradients[1]))
    start_totals = tuple((jnp.zeros(param.shape, jnp.float32) for param in params))
    totals, outputs = lax.scan(per_latent, start_totals, (tokens, condition, cotangent))
    result, grad_tokens, grad_condition = outputs
    return (result, grad_tokens, grad_condition, totals[0], totals[1], totals[2], totals[3], totals[4], totals[5], totals[6], totals[7], totals[8], totals[9])
```

```python
import functools
import math

import jax
import jax.numpy as jnp
from jax import lax
from jax.experimental import pallas as pl
from jax.experimental.pallas import tpu as pltpu
from jax.sharding import PartitionSpec as P

HD = 64
PAIR = 2 * HD
LOG2E = 1.4426950408889634
epsilon = 1e-06
f32 = jnp.float32
bf16 = jnp.bfloat16

NT = (((1,), (1,)), ((), ()))
NN = (((1,), (0,)), ((), ()))


def dot(a, b, dims=NN):
    return lax.dot_general(a, b, dims, preferred_element_type=f32)


def head_parts(block):
    lane = lax.broadcasted_iota(jnp.int32, block.shape, 1)
    zero = jnp.zeros_like(block)
    return [jnp.where(lane < HD, block, zero), jnp.where(lane < HD, zero, block)]


def attend_kernel(chunk, q_ref, k_ref, v_ref, o_ref, lse_ref):
    keys = k_ref[0]
    values_t = v_ref[0].T
    factor = LOG2E / math.sqrt(HD)

    def step(i, carry):
        rows = pl.ds(pl.multiple_of(i * chunk, chunk), chunk)
        parts = []
        for h, queries in enumerate(head_parts(q_ref[0, rows, :])):
            scores = dot(keys, queries, NT) * factor
            top = jnp.max(scores, axis=0, keepdims=True)
            shifted = jnp.exp2(scores - top)
            total = jnp.sum(shifted, axis=0, keepdims=True)
            out = dot(values_t[h * HD : (h + 1) * HD], shifted.astype(bf16))
            parts.append(out * (1.0 / total))
            lse_ref[0, 0, h : h + 1, rows] = top + jnp.log2(total)
        o_ref[0, rows, :] = jnp.concatenate(parts, 0).T.astype(bf16)
        return carry

    lax.fori_loop(0, q_ref.shape[1] // chunk, step, 0)


def attend(qkv, width):
    latents, length, _ = qkv.shape
    pairs = width // PAIR
    chunk = min(256, length)
    block = lambda at: pl.BlockSpec((1, length, PAIR), lambda l, p: (l, 0, at * pairs + p))
    elements = latents * length * length * (width // HD)
    return pl.pallas_call(
        functools.partial(attend_kernel, chunk),
        grid=(latents, pairs),
        in_specs=[block(0), block(1), block(2)],
        out_specs=[
            pl.BlockSpec((1, length, PAIR), lambda l, p: (l, 0, p)),
            pl.BlockSpec((1, 1, 2, length), lambda l, p: (l, p, 0, 0)),
        ],
        out_shape=[
            jax.ShapeDtypeStruct((latents, length, width), bf16),
            jax.ShapeDtypeStruct((latents, pairs, 2, length), f32),
        ],
        compiler_params=pltpu.CompilerParams(vmem_limit_bytes=40 * 2**20),
        cost_estimate=pl.CostEstimate(
            flops=elements * HD * 8, bytes_accessed=qkv.size * 3, transcendentals=elements
        ),
        name="attend",
    )(qkv, qkv, qkv)


def attend_back_kernel(chunk, q_ref, k_ref, v_ref, do_ref, lse_ref, g_ref, dq_s, dk_s, dv_s):
    which = pl.program_id(2)
    inverse = 1.0 / math.sqrt(HD)

    @pl.when(which == 0)
    def _():
        keys = k_ref[0]
        values = v_ref[0]
        keys_t = keys.T
        dk_s[...] = jnp.zeros_like(dk_s)
        dv_s[...] = jnp.zeros_like(dv_s)

        def step(i, carry):
            rows = pl.ds(pl.multiple_of(i * chunk, chunk), chunk)
            queries = head_parts(q_ref[0, rows, :])
            grads = head_parts(do_ref[0, rows, :])
            parts = []
            for h in range(2):
                scores = dot(keys, queries[h], NT) * (LOG2E * inverse)
                probs = jnp.exp2(scores - lse_ref[0, 0, h : h + 1, rows])
                g_probs = dot(values, grads[h], NT)
                delta = jnp.sum(probs * g_probs, axis=0, keepdims=True)
                g_scores = (probs * (g_probs - delta)).astype(bf16)
                dv_s[...] += dot(probs.astype(bf16), grads[h])
                dk_s[...] += dot(g_scores, queries[h])
                parts.append(dot(keys_t[h * HD : (h + 1) * HD], g_scores))
            dq_s[rows, :] = (jnp.concatenate(parts, 0).T * inverse).astype(bf16)
            return carry

        lax.fori_loop(0, q_ref.shape[1] // chunk, step, 0)
        g_ref[0] = dq_s[...]

    @pl.when(which == 1)
    def _():
        g_ref[0] = (dk_s[...] * inverse).astype(bf16)

    @pl.when(which == 2)
    def _():
        g_ref[0] = dv_s[...].astype(bf16)


def attend_back(qkv, g_attended, lse):
    latents, length, width = g_attended.shape
    pairs = width // PAIR
    chunk = min(256, length)
    block = lambda at: pl.BlockSpec((1, length, PAIR), lambda l, p, w: (l, 0, at * pairs + p))
    elements = latents * length * length * (width // HD)
    return pl.pallas_call(
        functools.partial(attend_back_kernel, chunk),
        grid=(latents, pairs, 3),
        in_specs=[
            block(0),
            block(1),
            block(2),
            block(0),
            pl.BlockSpec((1, 1, 2, length), lambda l, p, w: (l, p, 0, 0)),
        ],
        out_specs=pl.BlockSpec((1, length, PAIR), lambda l, p, w: (l, 0, w * pairs + p)),
        out_shape=jax.ShapeDtypeStruct((latents, length, 3 * width), bf16),
        scratch_shapes=[
            pltpu.VMEM((length, PAIR), bf16),
            pltpu.VMEM((length, PAIR), f32),
            pltpu.VMEM((length, PAIR), f32),
        ],
        compiler_params=pltpu.CompilerParams(vmem_limit_bytes=40 * 2**20),
        cost_estimate=pl.CostEstimate(
            flops=elements * HD * 20, bytes_accessed=qkv.size * 4, transcendentals=elements
        ),
        name="attend_back",
    )(qkv, qkv, qkv, g_attended, lse)


def modulate(residual, shift, scale):
    average = jnp.mean(residual, -1, keepdims=True)
    centred = residual - average
    spread = jnp.mean(centred * centred, -1, keepdims=True)
    return centred * lax.rsqrt(spread + epsilon) * (1.0 + scale[:, None, :]) + shift[:, None, :]


def gelu_tanh(values):
    return jax.nn.gelu(values, approximate=True)


def swap_in(x, parts):
    if parts == 1:
        return x
    if parts != 2:
        return lax.all_to_all(x, "seq", split_axis=0, concat_axis=1, tiled=True)
    here = lax.axis_index("seq")
    own = x.shape[0] // 2
    mine = lax.dynamic_slice_in_dim(x, here * own, own, 0)
    other = lax.dynamic_slice_in_dim(x, (1 - here) * own, own, 0)
    return jnp.concatenate([mine, lax.ppermute(other, "seq", [(0, 1), (1, 0)])], 1)


def swap_out(x, parts):
    if parts == 1:
        return x
    if parts != 2:
        sent = lax.all_to_all(x.astype(bf16), "seq", split_axis=1, concat_axis=0, tiled=True)
        return sent.astype(x.dtype)
    here = lax.axis_index("seq")
    rows = x.shape[1] // 2
    mine = x[:, :rows]
    other = lax.ppermute(x[:, rows:].astype(bf16), "seq", [(0, 1), (1, 0)]).astype(x.dtype)
    return jnp.where(
        here == 0, jnp.concatenate([mine, other], 0), jnp.concatenate([other, mine], 0)
    )


def gather_rows(x):
    return lax.all_gather(x, "shard", axis=0, tiled=True)


def seq_sum(x, parts):
    if parts == 2:
        return x.astype(f32) + lax.ppermute(x, "seq", [(0, 1), (1, 0)]).astype(f32)
    return lax.psum(x.astype(f32), "seq")


def scatter_rows(g, parts):
    own = lax.psum_scatter(g.astype(bf16), "shard", scatter_dimension=0, tiled=True)
    return seq_sum(own, parts)


def shards(
    shape,
    tokens,
    condition,
    cotangent,
    ada_weight,
    ada_bias,
    qkv_weight,
    qv_bias,
    proj_weight,
    proj_bias,
    up_weight,
    up_bias,
    down_weight,
    down_bias,
):
    n, parts = shape["shard"], shape["seq"]
    shard, seq = lax.axis_index("shard"), lax.axis_index("seq")
    latents, local_rows, width = tokens.shape
    own = latents // parts
    columns = ada_weight.shape[0]
    ff = down_weight.shape[0] * n

    biases = (qv_bias, proj_bias, up_bias, down_bias)
    sizes = [b.shape[0] for b in biases]
    w_qkv = gather_rows(qkv_weight)
    tokens_own = swap_in(tokens, parts)
    all_biases = lax.all_gather(jnp.concatenate(biases), "shard", axis=0, tiled=False).astype(f32)
    offsets = [sum(sizes[:i]) for i in range(5)]
    b_qv, b_proj, b_up, b_down = [
        all_biases[:, offsets[i] : offsets[i + 1]].reshape(-1) for i in range(4)
    ]

    cond_float = condition.astype(f32)
    cond_act = jax.nn.silu(cond_float).astype(bf16)
    cond_cols = lax.all_to_all(
        cond_act.reshape(latents, n, columns).transpose(1, 0, 2), "shard", 0, 0, tiled=True
    )
    cond_cols = cond_cols.reshape(n, latents, columns)
    cond_block = lax.dynamic_slice_in_dim(cond_cols, seq * own, own, 1).reshape(n * own, columns)
    partial = dot(cond_block, ada_weight)
    span = ada_bias.shape[0]
    owned = lax.broadcasted_iota(jnp.int32, (1, n, 1), 1) == shard
    bias_row = jnp.where(owned, ada_bias.astype(f32)[None, None, :], 0.0).reshape(1, n * span)
    partial = (partial + bias_row).reshape(n, own * n * span)
    arrived = lax.all_to_all(partial, "shard", 0, 0, tiled=True)
    modulation = jnp.sum(arrived, axis=0).reshape(own, n * span)
    shift_one, scale_one, gate_one, shift_two, scale_two, gate_two = jnp.split(
        modulation, 6, axis=1
    )

    w_proj = gather_rows(proj_weight)
    w_up = gather_rows(up_weight)
    w_down = gather_rows(down_weight)
    cot_own = swap_in(cotangent, parts)

    residual = tokens_own.astype(f32)
    normed_one = modulate(residual, shift_one, scale_one).astype(bf16)
    zero = jnp.zeros((width,), f32)
    qkv_bias = jnp.concatenate([b_qv[:width], zero, b_qv[width:]])
    qkv = (
        jnp.einsum("btd,de->bte", normed_one, w_qkv, preferred_element_type=f32) + qkv_bias
    ).astype(bf16)
    attended, lse = attend(qkv, width)
    branch = jnp.einsum("bte,ed->btd", attended, w_proj, preferred_element_type=f32) + b_proj
    middle = residual + gate_one[:, None, :] * branch
    normed_two = modulate(middle, shift_two, scale_two).astype(bf16)
    hidden = jnp.einsum("btd,df->btf", normed_two, w_up, preferred_element_type=f32) + b_up
    active = gelu_tanh(hidden).astype(bf16)
    output = jnp.einsum("btf,fd->btd", active, w_down, preferred_element_type=f32) + b_down
    result = swap_out((middle + gate_two[:, None, :] * output).astype(bf16), parts)

    grad_result = cot_own.astype(f32)
    grad_output = (gate_two[:, None, :] * grad_result).astype(bf16)
    grad_gate_two = jnp.sum(grad_result * output, axis=1)
    grad_down_weight = scatter_rows(
        jnp.einsum("btf,btd->fd", active, grad_output, preferred_element_type=f32), parts
    )
    grad_down_bias = jnp.sum(grad_output, axis=(0, 1), dtype=f32)
    grad_active = jnp.einsum("btd,fd->btf", grad_output, w_down, preferred_element_type=f32)
    unused, gelu_back = jax.vjp(gelu_tanh, hidden)
    grad_hidden = gelu_back(grad_active)[0].astype(bf16)
    grad_up_weight = scatter_rows(
        jnp.einsum("btd,btf->df", normed_two, grad_hidden, preferred_element_type=f32), parts
    )
    grad_up_bias = jnp.sum(grad_hidden, axis=(0, 1), dtype=f32)
    grad_normed_two = jnp.einsum("btf,df->btd", grad_hidden, w_up, preferred_element_type=f32)
    unused, norm_back_two = jax.vjp(modulate, middle, shift_two, scale_two)
    grad_middle, grad_shift_two, grad_scale_two = norm_back_two(grad_normed_two)
    grad_middle = grad_middle + grad_result
    grad_branch = (gate_one[:, None, :] * grad_middle).astype(bf16)
    grad_gate_one = jnp.sum(grad_middle * branch, axis=1)
    grad_proj_weight = scatter_rows(
        jnp.einsum("bte,btd->ed", attended, grad_branch, preferred_element_type=f32), parts
    )
    grad_proj_bias = jnp.sum(grad_branch, axis=(0, 1), dtype=f32)
    grad_attended = jnp.einsum(
        "btd,ed->bte", grad_branch, w_proj, preferred_element_type=f32
    ).astype(bf16)
    grad_qkv = attend_back(qkv, grad_attended, lse)
    grad_qkv_weight = scatter_rows(
        jnp.einsum("btd,bte->de", normed_one, grad_qkv, preferred_element_type=f32), parts
    )
    column_sums = jnp.sum(grad_qkv, axis=(0, 1), dtype=f32)
    grad_qv_bias = jnp.concatenate([column_sums[:width], column_sums[2 * width :]])
    grad_normed_one = jnp.einsum("bte,de->btd", grad_qkv, w_qkv, preferred_element_type=f32)
    unused, norm_back_one = jax.vjp(modulate, residual, shift_one, scale_one)
    grad_input, grad_shift_one, grad_scale_one = norm_back_one(grad_normed_one)
    grad_tokens = swap_out(grad_input + grad_middle, parts)

    grad_modulation = jnp.concatenate(
        [
            grad_shift_one,
            grad_scale_one,
            grad_gate_one,
            grad_shift_two,
            grad_scale_two,
            grad_gate_two,
        ],
        axis=1,
    ).astype(bf16)
    bias_grads = jnp.concatenate(
        [
            g.reshape(n, -1)
            for g in (grad_qv_bias, grad_proj_bias, grad_up_bias, grad_down_bias)
        ],
        axis=1,
    ).astype(bf16)
    total = sum(sizes)
    sent = jnp.concatenate([grad_modulation.reshape(-1), bias_grads.reshape(-1)])
    everyone = lax.all_gather(sent, ("shard", "seq"), axis=0, tiled=False)
    everyone = everyone.reshape(n * parts, -1)
    all_modulation = everyone[:, : own * n * span].reshape(n * latents, n * span)
    own_biases = jnp.sum(
        lax.dynamic_slice_in_dim(everyone, own * n * span + shard * total, total, 1).astype(f32),
        axis=0,
    )
    grad_qv, grad_proj, grad_up, grad_down = [
        own_biases[offsets[i] : offsets[i + 1]] for i in range(4)
    ]
    grad_ada_weight = lax.dot_general(
        cond_cols.reshape(n * latents, columns),
        all_modulation,
        (((0,), (0,)), ((), ())),
        preferred_element_type=f32,
    )
    grad_ada_bias = jnp.sum(
        lax.dynamic_slice_in_dim(all_modulation, shard * span, span, 1).astype(f32), axis=0
    )
    grad_cond_cols = dot(all_modulation, ada_weight, NT).reshape(n, latents * columns)
    grad_cond_act = lax.all_to_all(grad_cond_cols, "shard", 0, 0, tiled=True)
    grad_cond_act = (
        grad_cond_act.reshape(n, latents, columns).transpose(1, 0, 2).reshape(latents, width)
    )
    unused, silu_back = jax.vjp(jax.nn.silu, cond_float)
    grad_condition = silu_back(grad_cond_act)[0]
    return (
        result,
        grad_tokens,
        grad_condition,
        grad_ada_weight,
        grad_ada_bias,
        grad_qkv_weight,
        grad_qv,
        grad_proj_weight,
        grad_proj,
        grad_up_weight,
        grad_up,
        grad_down_weight,
        grad_down,
    )


def solution(mesh):
    rows, flat = P("shard", None), P("shard")
    split = P("shard", "seq", None)
    in_specs = (split, rows, split) + (rows, flat) * 5
    out_specs = (split, split, rows) + (rows, flat) * 5
    body = functools.partial(shards, dict(mesh.shape))
    return jax.shard_map(
        body, mesh=mesh, in_specs=in_specs, out_specs=out_specs, check_vma=False
    )
```

```python
import functools
import math

import jax
import jax.numpy as jnp
from jax import lax
from jax.experimental import pallas as pl
from jax.experimental.pallas import tpu as pltpu
from jax.sharding import PartitionSpec as P

HD = 64
PAIR = 2 * HD
LOG2E = 1.4426950408889634
epsilon = 1e-06
f32 = jnp.float32
bf16 = jnp.bfloat16

NT = (((1,), (1,)), ((), ()))
NN = (((1,), (0,)), ((), ()))


def dot(a, b, dims=NN):
    return lax.dot_general(a, b, dims, preferred_element_type=f32)


def head_parts(block):
    lane = lax.broadcasted_iota(jnp.int32, block.shape, 1)
    zero = jnp.zeros_like(block)
    return [jnp.where(lane < HD, block, zero), jnp.where(lane < HD, zero, block)]


def attend_kernel(chunk, q_ref, k_ref, v_ref, o_ref, lse_ref):
    keys = k_ref[0]
    values_t = v_ref[0].T
    factor = LOG2E / math.sqrt(HD)

    def step(i, carry):
        rows = pl.ds(pl.multiple_of(i * chunk, chunk), chunk)
        parts = []
        for h, queries in enumerate(head_parts(q_ref[0, rows, :])):
            scores = dot(keys, queries, NT) * factor
            top = jnp.max(scores, axis=0, keepdims=True)
            shifted = jnp.exp2(scores - top)
            total = jnp.sum(shifted, axis=0, keepdims=True)
            out = dot(values_t[h * HD : (h + 1) * HD], shifted.astype(bf16))
            parts.append(out * (1.0 / total))
            lse_ref[0, 0, h : h + 1, rows] = top + jnp.log2(total)
        o_ref[0, rows, :] = jnp.concatenate(parts, 0).T.astype(bf16)
        return carry

    lax.fori_loop(0, q_ref.shape[1] // chunk, step, 0)


def attend(qkv, width):
    latents, length, _ = qkv.shape
    pairs = width // PAIR
    chunk = min(256, length)
    block = lambda at: pl.BlockSpec((1, length, PAIR), lambda l, p: (l, 0, at * pairs + p))
    elements = latents * length * length * (width // HD)
    return pl.pallas_call(
        functools.partial(attend_kernel, chunk),
        grid=(latents, pairs),
        in_specs=[block(0), block(1), block(2)],
        out_specs=[
            pl.BlockSpec((1, length, PAIR), lambda l, p: (l, 0, p)),
            pl.BlockSpec((1, 1, 2, length), lambda l, p: (l, p, 0, 0)),
        ],
        out_shape=[
            jax.ShapeDtypeStruct((latents, length, width), bf16),
            jax.ShapeDtypeStruct((latents, pairs, 2, length), f32),
        ],
        compiler_params=pltpu.CompilerParams(vmem_limit_bytes=40 * 2**20),
        cost_estimate=pl.CostEstimate(
            flops=elements * HD * 8, bytes_accessed=qkv.size * 3, transcendentals=elements
        ),
        name="attend",
    )(qkv, qkv, qkv)


def attend_back_kernel(chunk, q_ref, k_ref, v_ref, do_ref, lse_ref, g_ref, dq_s, dk_s, dv_s):
    which = pl.program_id(2)
    inverse = 1.0 / math.sqrt(HD)

    @pl.when(which == 0)
    def _():
        keys = k_ref[0]
        values = v_ref[0]
        keys_t = keys.T
        dk_s[...] = jnp.zeros_like(dk_s)
        dv_s[...] = jnp.zeros_like(dv_s)

        def step(i, carry):
            rows = pl.ds(pl.multiple_of(i * chunk, chunk), chunk)
            queries = head_parts(q_ref[0, rows, :])
            grads = head_parts(do_ref[0, rows, :])
            parts = []
            for h in range(2):
                scores = dot(keys, queries[h], NT) * (LOG2E * inverse)
                probs = jnp.exp2(scores - lse_ref[0, 0, h : h + 1, rows])
                g_probs = dot(values, grads[h], NT)
                delta = jnp.sum(probs * g_probs, axis=0, keepdims=True)
                g_scores = (probs * (g_probs - delta)).astype(bf16)
                dv_s[...] += dot(probs.astype(bf16), grads[h])
                dk_s[...] += dot(g_scores, queries[h])
                parts.append(dot(keys_t[h * HD : (h + 1) * HD], g_scores))
            dq_s[rows, :] = (jnp.concatenate(parts, 0).T * inverse).astype(bf16)
            return carry

        lax.fori_loop(0, q_ref.shape[1] // chunk, step, 0)
        g_ref[0] = dq_s[...]

    @pl.when(which == 1)
    def _():
        g_ref[0] = (dk_s[...] * inverse).astype(bf16)

    @pl.when(which == 2)
    def _():
        g_ref[0] = dv_s[...].astype(bf16)


def attend_back(qkv, g_attended, lse):
    latents, length, width = g_attended.shape
    pairs = width // PAIR
    chunk = min(256, length)
    block = lambda at: pl.BlockSpec((1, length, PAIR), lambda l, p, w: (l, 0, at * pairs + p))
    elements = latents * length * length * (width // HD)
    return pl.pallas_call(
        functools.partial(attend_back_kernel, chunk),
        grid=(latents, pairs, 3),
        in_specs=[
            block(0),
            block(1),
            block(2),
            block(0),
            pl.BlockSpec((1, 1, 2, length), lambda l, p, w: (l, p, 0, 0)),
        ],
        out_specs=pl.BlockSpec((1, length, PAIR), lambda l, p, w: (l, 0, w * pairs + p)),
        out_shape=jax.ShapeDtypeStruct((latents, length, 3 * width), bf16),
        scratch_shapes=[
            pltpu.VMEM((length, PAIR), bf16),
            pltpu.VMEM((length, PAIR), f32),
            pltpu.VMEM((length, PAIR), f32),
        ],
        compiler_params=pltpu.CompilerParams(vmem_limit_bytes=40 * 2**20),
        cost_estimate=pl.CostEstimate(
            flops=elements * HD * 20, bytes_accessed=qkv.size * 4, transcendentals=elements
        ),
        name="attend_back",
    )(qkv, qkv, qkv, g_attended, lse)


def modulate(residual, shift, scale):
    average = jnp.mean(residual, -1, keepdims=True)
    centred = residual - average
    spread = jnp.mean(centred * centred, -1, keepdims=True)
    return centred * lax.rsqrt(spread + epsilon) * (1.0 + scale[:, None, :]) + shift[:, None, :]


def gelu_tanh(values):
    return jax.nn.gelu(values, approximate=True)


def swap_in(x, parts):
    if parts == 1:
        return x
    if parts != 2:
        return lax.all_to_all(x, "seq", split_axis=0, concat_axis=1, tiled=True)
    here = lax.axis_index("seq")
    own = x.shape[0] // 2
    mine = lax.dynamic_slice_in_dim(x, here * own, own, 0)
    other = lax.dynamic_slice_in_dim(x, (1 - here) * own, own, 0)
    return jnp.concatenate([mine, lax.ppermute(other, "seq", [(0, 1), (1, 0)])], 1)


def swap_out(x, parts):
    if parts == 1:
        return x
    if parts != 2:
        sent = lax.all_to_all(x.astype(bf16), "seq", split_axis=1, concat_axis=0, tiled=True)
        return sent.astype(x.dtype)
    here = lax.axis_index("seq")
    rows = x.shape[1] // 2
    mine = x[:, :rows]
    other = lax.ppermute(x[:, rows:].astype(bf16), "seq", [(0, 1), (1, 0)]).astype(x.dtype)
    return jnp.where(
        here == 0, jnp.concatenate([mine, other], 0), jnp.concatenate([other, mine], 0)
    )


def gather_rows(x):
    return lax.all_gather(x, "shard", axis=0, tiled=True)


def seq_sum(x, parts):
    if parts == 2:
        return x.astype(f32) + lax.ppermute(x, "seq", [(0, 1), (1, 0)]).astype(f32)
    return lax.psum(x.astype(f32), "seq")


def scatter_rows(g, parts):
    own = lax.psum_scatter(g.astype(bf16), "shard", scatter_dimension=0, tiled=True)
    return seq_sum(own, parts)


def shards(
    shape,
    tokens,
    condition,
    cotangent,
    ada_weight,
    ada_bias,
    qkv_weight,
    qv_bias,
    proj_weight,
    proj_bias,
    up_weight,
    up_bias,
    down_weight,
    down_bias,
):
    n, parts = shape["shard"], shape["seq"]
    shard, seq = lax.axis_index("shard"), lax.axis_index("seq")
    latents, local_rows, width = tokens.shape
    own = latents // parts
    columns = ada_weight.shape[0]
    ff = down_weight.shape[0] * n

    biases = (qv_bias, proj_bias, up_bias, down_bias)
    sizes = [b.shape[0] for b in biases]
    w_qkv = gather_rows(qkv_weight)
    tokens_own = swap_in(tokens, parts)
    all_biases = lax.all_gather(jnp.concatenate(biases), "shard", axis=0, tiled=False).astype(f32)
    offsets = [sum(sizes[:i]) for i in range(5)]
    b_qv, b_proj, b_up, b_down = [
        all_biases[:, offsets[i] : offsets[i + 1]].reshape(-1) for i in range(4)
    ]

    cond_float = condition.astype(f32)
    cond_act = jax.nn.silu(cond_float).astype(bf16)
    cond_cols = lax.all_to_all(
        cond_act.reshape(latents, n, columns).transpose(1, 0, 2), "shard", 0, 0, tiled=True
    )
    cond_cols = cond_cols.reshape(n, latents, columns)
    cond_block = lax.dynamic_slice_in_dim(cond_cols, seq * own, own, 1).reshape(n * own, columns)
    partial = dot(cond_block, ada_weight)
    span = ada_bias.shape[0]
    owned = lax.broadcasted_iota(jnp.int32, (1, n, 1), 1) == shard
    bias_row = jnp.where(owned, ada_bias.astype(f32)[None, None, :], 0.0).reshape(1, n * span)
    partial = (partial + bias_row).reshape(n, own * n * span)
    arrived = lax.all_to_all(partial, "shard", 0, 0, tiled=True)
    modulation = jnp.sum(arrived, axis=0).reshape(own, n * span)
    shift_one, scale_one, gate_one, shift_two, scale_two, gate_two = jnp.split(
        modulation, 6, axis=1
    )

    w_proj = gather_rows(proj_weight)
    w_up = gather_rows(up_weight)
    w_down = gather_rows(down_weight)
    cot_own = swap_in(cotangent, parts)

    residual = tokens_own.astype(f32)
    normed_one = modulate(residual, shift_one, scale_one).astype(bf16)
    zero = jnp.zeros((width,), f32)
    qkv_bias = jnp.concatenate([b_qv[:width], zero, b_qv[width:]])
    qkv = (
        jnp.einsum("btd,de->bte", normed_one, w_qkv, preferred_element_type=f32) + qkv_bias
    ).astype(bf16)
    attended, lse = attend(qkv, width)
    branch = jnp.einsum("bte,ed->btd", attended, w_proj, preferred_element_type=f32) + b_proj
    middle = residual + gate_one[:, None, :] * branch
    normed_two = modulate(middle, shift_two, scale_two).astype(bf16)
    hidden = jnp.einsum("btd,df->btf", normed_two, w_up, preferred_element_type=f32) + b_up
    active = gelu_tanh(hidden).astype(bf16)
    output = jnp.einsum("btf,fd->btd", active, w_down, preferred_element_type=f32) + b_down
    result = swap_out((middle + gate_two[:, None, :] * output).astype(bf16), parts)

    grad_result = cot_own.astype(f32)
    grad_output = (gate_two[:, None, :] * grad_result).astype(bf16)
    grad_gate_two = jnp.sum(grad_result * output, axis=1)
    partial_down = jnp.einsum(
        "btf,btd->fd", active, grad_output, preferred_element_type=f32
    ).astype(bf16)
    grad_output, partial_down = lax.optimization_barrier((grad_output, partial_down))
    grad_down_weight = scatter_rows(partial_down, parts)
    grad_down_bias = jnp.sum(grad_output, axis=(0, 1), dtype=f32)
    grad_active = jnp.einsum("btd,fd->btf", grad_output, w_down, preferred_element_type=f32)
    unused, gelu_back = jax.vjp(gelu_tanh, hidden)
    grad_hidden = gelu_back(grad_active)[0].astype(bf16)
    partial_up = jnp.einsum(
        "btd,btf->df", normed_two, grad_hidden, preferred_element_type=f32
    ).astype(bf16)
    grad_hidden, partial_up = lax.optimization_barrier((grad_hidden, partial_up))
    grad_up_weight = scatter_rows(partial_up, parts)
    grad_up_bias = jnp.sum(grad_hidden, axis=(0, 1), dtype=f32)
    grad_normed_two = jnp.einsum("btf,df->btd", grad_hidden, w_up, preferred_element_type=f32)
    unused, norm_back_two = jax.vjp(modulate, middle, shift_two, scale_two)
    grad_middle, grad_shift_two, grad_scale_two = norm_back_two(grad_normed_two)
    grad_middle = grad_middle + grad_result
    grad_branch = (gate_one[:, None, :] * grad_middle).astype(bf16)
    grad_gate_one = jnp.sum(grad_middle * branch, axis=1)
    partial_proj = jnp.einsum(
        "bte,btd->ed", attended, grad_branch, preferred_element_type=f32
    ).astype(bf16)
    grad_branch, partial_proj = lax.optimization_barrier((grad_branch, partial_proj))
    grad_proj_weight = scatter_rows(partial_proj, parts)
    grad_proj_bias = jnp.sum(grad_branch, axis=(0, 1), dtype=f32)
    grad_attended = jnp.einsum(
        "btd,ed->bte", grad_branch, w_proj, preferred_element_type=f32
    ).astype(bf16)
    grad_attended, grad_down_weight = lax.optimization_barrier((grad_attended, grad_down_weight))
    grad_qkv = attend_back(qkv, grad_attended, lse)
    grad_qkv_weight = scatter_rows(
        jnp.einsum("btd,bte->de", normed_one, grad_qkv, preferred_element_type=f32), parts
    )
    column_sums = jnp.sum(grad_qkv, axis=(0, 1), dtype=f32)
    grad_qv_bias = jnp.concatenate([column_sums[:width], column_sums[2 * width :]])
    grad_normed_one = jnp.einsum("bte,de->btd", grad_qkv, w_qkv, preferred_element_type=f32)
    unused, norm_back_one = jax.vjp(modulate, residual, shift_one, scale_one)
    grad_input, grad_shift_one, grad_scale_one = norm_back_one(grad_normed_one)
    grad_tokens = swap_out(grad_input + grad_middle, parts)

    grad_modulation = jnp.concatenate(
        [
            grad_shift_one,
            grad_scale_one,
            grad_gate_one,
            grad_shift_two,
            grad_scale_two,
            grad_gate_two,
        ],
        axis=1,
    ).astype(bf16)
    bias_grads = jnp.concatenate(
        [
            g.reshape(n, -1)
            for g in (grad_qv_bias, grad_proj_bias, grad_up_bias, grad_down_bias)
        ],
        axis=1,
    ).astype(bf16)
    total = sum(sizes)
    sent = jnp.concatenate([grad_modulation.reshape(-1), bias_grads.reshape(-1)])
    everyone = lax.all_gather(sent, ("shard", "seq"), axis=0, tiled=False)
    everyone = everyone.reshape(n * parts, -1)
    all_modulation = everyone[:, : own * n * span].reshape(n * latents, n * span)
    own_biases = jnp.sum(
        lax.dynamic_slice_in_dim(everyone, own * n * span + shard * total, total, 1).astype(f32),
        axis=0,
    )
    grad_qv, grad_proj, grad_up, grad_down = [
        own_biases[offsets[i] : offsets[i + 1]] for i in range(4)
    ]
    grad_ada_weight = lax.dot_general(
        cond_cols.reshape(n * latents, columns),
        all_modulation,
        (((0,), (0,)), ((), ())),
        preferred_element_type=f32,
    )
    grad_ada_bias = jnp.sum(
        lax.dynamic_slice_in_dim(all_modulation, shard * span, span, 1).astype(f32), axis=0
    )
    grad_cond_cols = dot(all_modulation, ada_weight, NT).reshape(n, latents * columns)
    grad_cond_act = lax.all_to_all(grad_cond_cols, "shard", 0, 0, tiled=True)
    grad_cond_act = (
        grad_cond_act.reshape(n, latents, columns).transpose(1, 0, 2).reshape(latents, width)
    )
    unused, silu_back = jax.vjp(jax.nn.silu, cond_float)
    grad_condition = silu_back(grad_cond_act)[0]
    return (
        result,
        grad_tokens,
        grad_condition,
        grad_ada_weight,
        grad_ada_bias,
        grad_qkv_weight,
        grad_qv,
        grad_proj_weight,
        grad_proj,
        grad_up_weight,
        grad_up,
        grad_down_weight,
        grad_down,
    )


def solution(mesh):
    rows, flat = P("shard", None), P("shard")
    split = P("shard", "seq", None)
    in_specs = (split, rows, split) + (rows, flat) * 5
    out_specs = (split, split, rows) + (rows, flat) * 5
    body = functools.partial(shards, dict(mesh.shape))
    return jax.shard_map(
        body, mesh=mesh, in_specs=in_specs, out_specs=out_specs, check_vma=False
    )
```
